32 devices in a mesh: groups: 2 (over y), dp: 4 (over z), tile: 4 (over x, core).
Axes of the slice: x: 2, y: 2, z: 4, core: 2. Of those that a mesh axis runs over, the one named last changes fastest.
Arguments:
- features: bfloat16 [8, 32, 128, 1024], P(('groups', 'dp'), 'tile'), parts along dimension 0, may hold values from -18 to 18
- cotangent: bfloat16 [8, 32, 128, 512], P(('groups', 'dp'), 'tile'), parts along dimension 0, may hold values from -6 to 6
- weight_first: bfloat16 [1024, 512], replicated, may hold values from -0.1875 to 0.1875
- weight_second: bfloat16 [512, 512], replicated, may hold values from -0.25 to 0.25
- cluster_id: int32 [8, 32, 128], P(('groups', 'dp'), 'tile'), parts along dimension 0, may hold values from 0 to 2047, as said below
- cluster_size: int32 [8, 2048], P(('groups', 'dp')), parts along dimension 0, may hold values from 1 to 3, as said below
Outputs:
- grad_features: bfloat16 [8, 32, 128, 1024], P(('groups', 'dp'), 'tile'), parts along dimension 0
- grad_first: float32 [2048, 512], P('groups'), parts along dimension 0
- grad_second: float32 [1024, 512], P('groups'), parts along dimension 0
The draws below stay inside these ranges and needn't reach their ends.
There are 2 independent parts, one for each index of `groups`. The reference program is written for one: setup_inputs(seed, part) draws one part's arguments, and reference() takes and returns one part's arrays. A program takes and returns all parts, laid end to end along the dimension named above; an argument that names none is the same for every part. Nothing has to cross between parts.
Inputs may be any that keep to these rules, and one draw needn't show every extreme that they name: `cluster_id`: every one of the 2048 clusters has at least one tile in every slide. cluster_size[s, k] is the number of tiles of slide s whose cluster_id is k; in every slide some cluster reaches the maximum and some has a single tile.
All inputs are finite; a program needn't handle non-finite values.
Results may differ from the reference program's by a relative error of at most 0.011.
Values may be sent and summed in bfloat16 or wider, within the bound.
A program may use at most 128 MiB of HBM per device.

```python
import jax
import jax.numpy as jnp
from jax import lax

F_IN = 1024
F_HID = 512
F_OUT = 512
CLUSTERS = 2048
COLS = 128
NROWS = 32
SLIDES = 4


def cluster_layout(key):
    label_key, place_key = jax.random.split(key, 2)
    count = NROWS * COLS
    extra_total = count - CLUSTERS
    base = extra_total // CLUSTERS
    remain = extra_total % CLUSTERS
    ranks = jnp.arange(CLUSTERS, dtype=jnp.int32)
    rank_sizes = 1 + jnp.where(ranks < CLUSTERS // 2, 2 * base, 0) + jnp.where(ranks < remain, 1, 0)
    rank_sizes = rank_sizes.astype(jnp.int32)
    bounds = jnp.cumsum(rank_sizes).astype(jnp.int32)
    slot_rank = jnp.searchsorted(bounds, jnp.arange(count, dtype=jnp.int32), side='right').astype(jnp.int32)
    label_keys = jax.random.split(label_key, SLIDES)
    place_keys = jax.random.split(place_key, SLIDES)

    def one_slide(first_key, second_key):
        labels = jax.random.permutation(first_key, CLUSTERS).astype(jnp.int32)
        order = jax.random.permutation(second_key, count).astype(jnp.int32)
        slot_label = labels[slot_rank]
        members = jnp.zeros((count,), jnp.int32).at[order].set(slot_label)
        sizes = jnp.zeros((CLUSTERS,), jnp.int32).at[labels].set(rank_sizes)
        return (members, sizes)
    members, totals = jax.vmap(one_slide)(label_keys, place_keys)
    return (members.reshape(SLIDES, NROWS, COLS).astype(jnp.int32), totals.astype(jnp.int32))


def draw_cluster_id(key, part):
    return cluster_layout(key)[0]


def draw_cluster_size(key, part):
    return cluster_layout(key)[1]


def levels(key, shape, pieces, smallest, largest):
    factor_of = 1.0
    for position, blocks in pieces:
        steps = jax.random.uniform(jax.random.fold_in(jax.random.fold_in(key, 6), position), (blocks,), jnp.float32, smallest / len(pieces), largest / len(pieces))
        factor_of = factor_of * jnp.repeat(jnp.exp(steps), shape[position] // blocks).reshape((-1,) + (1,) * (len(shape) - 1 - position))
    return factor_of


def scatter_about(own_key, dims, scale, most, pieces=(), kind=jnp.bfloat16):
    drawn = scale * jax.random.normal(own_key, dims, jnp.float32)
    if pieces:
        drawn = drawn * levels(own_key, dims, pieces, -0.22, 0.18)
    return jnp.clip(drawn, -most, most).astype(kind)


def setup_inputs(seed: int = 0, part: int = 0) -> dict:
    streams_of = jax.random.split(jax.random.key(seed), 7)
    part_keys = jax.random.split(jax.random.fold_in(streams_of[6], part), 7)
    return {
        "features": scatter_about(part_keys[0], (SLIDES, NROWS, COLS, F_IN), 3.0, 18.0, ((0, 4), (1, 4))),
        "cotangent": scatter_about(part_keys[1], (SLIDES, NROWS, COLS, F_OUT), 1.0, 6.0, ((0, 4), (1, 4))),
        "weight_first": scatter_about(streams_of[2], (F_IN, F_HID), F_IN ** -0.5, 0.1875),
        "weight_second": scatter_about(streams_of[3], (F_HID, F_OUT), F_HID ** -0.5, 0.25),
        "cluster_id": draw_cluster_id(jax.random.fold_in(jax.random.fold_in(streams_of[6], part), 71), part),
        "cluster_size": draw_cluster_size(jax.random.fold_in(jax.random.fold_in(streams_of[6], part), 71), part),
    }


def boxsum(values):
    padded = jnp.pad(values, ((1, 1), (1, 1), (0, 0)))
    along = padded[:-2] + padded[1:-1] + padded[2:]
    return along[:, :-2] + along[:, 1:-1] + along[:, 2:]

def spread_table(row_total, col_total):
    row_index = jnp.arange(row_total)
    col_index = jnp.arange(col_total)
    row_part = 3.0 - (row_index == 0).astype(jnp.float32) - (row_index == row_total - 1).astype(jnp.float32)
    col_part = 3.0 - (col_index == 0).astype(jnp.float32) - (col_index == col_total - 1).astype(jnp.float32)
    return row_part[:, None] * col_part[None, :]

def propagate(values, members, member_sizes):
    width = values.shape[-1]
    spread = spread_table(NROWS, COLS)
    root = 1.0 / jnp.sqrt(spread + 1.0)
    scaled = (values.astype(jnp.float32) * root[..., None]).astype(jnp.bfloat16)
    spatial_mean = boxsum(scaled.astype(jnp.float32)) / spread[..., None]
    spatial = boxsum(spatial_mean)
    totals = jax.ops.segment_sum(scaled.reshape(-1, width).astype(jnp.float32), members.reshape(-1), num_segments=CLUSTERS)
    cluster_mean = (totals / member_sizes.astype(jnp.float32)[:, None]).astype(jnp.bfloat16)
    picked = jnp.take(cluster_mean, members.reshape(-1), axis=0).reshape(values.shape)
    return (root[..., None] * (spatial + picked.astype(jnp.float32))).astype(jnp.bfloat16)

def reference(features, cotangent, weight_first, weight_second, cluster_id, cluster_size):

    def one_slide(inputs):
        feats, cotan, members, member_sizes = inputs
        flat_in = feats.reshape(-1, F_IN)
        hidden_in = jnp.dot(flat_in, weight_first, preferred_element_type=jnp.float32).astype(jnp.bfloat16)
        pre_act = propagate(hidden_in.reshape(NROWS, COLS, F_HID), members, member_sizes)
        back_second = propagate(cotan, members, member_sizes)
        pre_flat = pre_act.reshape(-1, F_HID).astype(jnp.float32)
        sigma = jax.nn.sigmoid(pre_flat)
        activated = (pre_flat * sigma).astype(jnp.bfloat16)
        back_flat = back_second.reshape(-1, F_OUT)
        grad_second = jnp.dot(activated.T, back_flat, preferred_element_type=jnp.float32)
        upstream = jnp.dot(back_flat, weight_second.T, preferred_element_type=jnp.float32)
        grad_pre = (upstream * sigma * (1.0 + pre_flat * (1.0 - sigma))).astype(jnp.bfloat16)
        back_first = propagate(grad_pre.reshape(NROWS, COLS, F_HID), members, member_sizes)
        first_flat = back_first.reshape(-1, F_HID)
        grad_first = jnp.dot(flat_in.T, first_flat, preferred_element_type=jnp.float32)
        grad_feats = jnp.dot(first_flat, weight_first.T, preferred_element_type=jnp.float32).astype(jnp.bfloat16)
        return (grad_feats.reshape(NROWS, COLS, F_IN), grad_first, grad_second)
    grad_features, grad_firsts, grad_seconds = lax.map(one_slide, (features, cotangent, cluster_id, cluster_size))
    return (grad_features, lax.optimization_barrier(jnp.sum(grad_firsts, axis=0)), lax.optimization_barrier(jnp.sum(grad_seconds, axis=0)))
```

```python
import jax
import jax.numpy as jnp
from jax import lax
from jax.sharding import PartitionSpec as P


def extended(cells, sides, width):
    for axis, dim in sides:
        count = lax.axis_size(axis)
        ends = count - 1
        head = lax.slice_in_dim(cells, 0, width, axis=dim)
        tail = lax.slice_in_dim(cells, cells.shape[dim] - width, cells.shape[dim], axis=dim)
        cells = jnp.concatenate(
            [
                lax.ppermute(tail, axis, [(i, (i + 1) % count) for i in range(ends)]),
                cells,
                lax.ppermute(head, axis, [((i + 1) % count, i) for i in range(ends)]),
            ],
            axis=dim,
        )
    return cells


def rowbox(values):
    return values[:-2] + values[1:-1] + values[2:]


def colbox(values):
    padded = jnp.pad(values, ((0, 0), (1, 1), (0, 0)))
    return padded[:, :-2] + padded[:, 1:-1] + padded[:, 2:]


def spread_rows(global_rows, row_total, col_total):
    row_part = (
        3.0
        - (global_rows == 0).astype(jnp.float32)
        - (global_rows == row_total - 1).astype(jnp.float32)
    )
    col_index = jnp.arange(col_total)
    col_part = (
        3.0
        - (col_index == 0).astype(jnp.float32)
        - (col_index == col_total - 1).astype(jnp.float32)
    )
    return row_part[:, None] * col_part[None, :]


def propagate(values, same, count):
    band_rows, grid_cols, width = values.shape
    bands = lax.axis_size("tile")
    row_start = lax.axis_index("tile") * band_rows
    row_total = band_rows * bands
    global_rows = row_start + jnp.arange(band_rows)
    spread = spread_rows(global_rows, row_total, grid_cols)
    root = 1.0 / jnp.sqrt(spread + 1.0)
    scaled = (values.astype(jnp.float32) * root[..., None]).astype(jnp.bfloat16)
    padded = extended(scaled, (("tile", 0),), 1)
    spatial_mean = colbox(rowbox(padded.astype(jnp.float32))) / spread[..., None]
    widened = extended(spatial_mean, (("tile", 0),), 1)
    spatial = colbox(rowbox(widened))
    piece_values = lax.all_gather(scaled, "tile", axis=0, tiled=True)
    total = jnp.dot(
        same, piece_values.reshape(-1, width), preferred_element_type=jnp.float32
    )
    picked = (total / count[:, None]).astype(jnp.bfloat16).reshape(values.shape)
    return (root[..., None] * (spatial + picked.astype(jnp.float32))).astype(jnp.bfloat16)


def local(features, cotangent, weight_first, weight_second, cluster_id, cluster_size):
    feats = features[0]
    band_rows, grid_cols, in_width = feats.shape
    hidden_width = weight_first.shape[1]
    out_width = weight_second.shape[1]
    members = cluster_id[0].reshape(-1)
    every = lax.all_gather(members, "tile", axis=0, tiled=True)
    same = (members[:, None] == every[None, :]).astype(jnp.bfloat16)
    count = jnp.take(cluster_size[0], members).astype(jnp.float32)
    flat_in = feats.reshape(-1, in_width)
    hidden_in = jnp.dot(flat_in, weight_first, preferred_element_type=jnp.float32).astype(
        jnp.bfloat16
    )
    hidden_grid = hidden_in.reshape(band_rows, grid_cols, hidden_width)
    pre_act = propagate(hidden_grid, same, count)
    back_second = propagate(cotangent[0], same, count)
    pre_flat = pre_act.reshape(-1, hidden_width).astype(jnp.float32)
    sigma = jax.nn.sigmoid(pre_flat)
    activated = (pre_flat * sigma).astype(jnp.bfloat16)
    back_flat = back_second.reshape(-1, out_width)
    grad_second = lax.dot_general(
        activated, back_flat, (((0,), (0,)), ((), ())), preferred_element_type=jnp.float32
    )
    upstream = lax.dot_general(
        back_flat, weight_second, (((1,), (1,)), ((), ())), preferred_element_type=jnp.float32
    )
    grad_pre = (upstream * sigma * (1.0 + pre_flat * (1.0 - sigma))).astype(jnp.bfloat16)
    back_first = propagate(
        grad_pre.reshape(band_rows, grid_cols, hidden_width), same, count
    )
    first_flat = back_first.reshape(-1, hidden_width)
    grad_first = lax.dot_general(
        flat_in, first_flat, (((0,), (0,)), ((), ())), preferred_element_type=jnp.float32
    )
    grad_feats = lax.dot_general(
        first_flat, weight_first, (((1,), (1,)), ((), ())), preferred_element_type=jnp.float32
    ).astype(jnp.bfloat16)
    grad_first, grad_second = lax.psum(
        (grad_first.astype(jnp.bfloat16), grad_second.astype(jnp.bfloat16)), ("dp", "tile")
    )
    return (
        grad_feats.reshape(1, band_rows, grid_cols, in_width),
        grad_first.astype(jnp.float32),
        grad_second.astype(jnp.float32),
    )


def solution(mesh):
    in_specs = (
        P(("groups", "dp"), "tile", None, None),
        P(("groups", "dp"), "tile", None, None),
        P(),
        P(),
        P(("groups", "dp"), "tile", None),
        P(("groups", "dp"), None),
    )
    out_specs = (P(("groups", "dp"), "tile", None, None), P("groups", None), P("groups", None))
    return jax.shard_map(local, mesh=mesh, in_specs=in_specs, out_specs=out_specs, check_vma=False)
```

```python
import jax
import jax.numpy as jnp
from jax import lax
from jax.experimental import pallas as pl
from jax.experimental.pallas import tpu as pltpu
from jax.sharding import PartitionSpec as P


def extended(cells, sides, width):
    for axis, dim in sides:
        count = lax.axis_size(axis)
        ends = count - 1
        head = lax.slice_in_dim(cells, 0, width, axis=dim)
        tail = lax.slice_in_dim(cells, cells.shape[dim] - width, cells.shape[dim], axis=dim)
        cells = jnp.concatenate(
            [
                lax.ppermute(tail, axis, [(i, (i + 1) % count) for i in range(ends)]),
                cells,
                lax.ppermute(head, axis, [((i + 1) % count, i) for i in range(ends)]),
            ],
            axis=dim,
        )
    return cells


def rowbox(values):
    return values[:-2] + values[1:-1] + values[2:]


def colbox(values):
    padded = jnp.pad(values, ((0, 0), (1, 1), (0, 0)))
    return padded[:, :-2] + padded[:, 1:-1] + padded[:, 2:]


def spread_rows(global_rows, row_total, col_total):
    row_part = (
        3.0
        - (global_rows == 0).astype(jnp.float32)
        - (global_rows == row_total - 1).astype(jnp.float32)
    )
    col_index = jnp.arange(col_total)
    col_part = (
        3.0
        - (col_index == 0).astype(jnp.float32)
        - (col_index == col_total - 1).astype(jnp.float32)
    )
    return row_part[:, None] * col_part[None, :]


def propagate(values, same, count):
    band_rows, grid_cols, width = values.shape
    bands = lax.axis_size("tile")
    row_start = lax.axis_index("tile") * band_rows
    row_total = band_rows * bands
    global_rows = row_start + jnp.arange(band_rows)
    spread = spread_rows(global_rows, row_total, grid_cols)
    root = 1.0 / jnp.sqrt(spread + 1.0)
    scaled = (values.astype(jnp.float32) * root[..., None]).astype(jnp.bfloat16)
    padded = extended(scaled, (("tile", 0),), 1)
    spatial_mean = colbox(rowbox(padded.astype(jnp.float32))) / spread[..., None]
    widened = extended(spatial_mean, (("tile", 0),), 1)
    spatial = colbox(rowbox(widened))
    piece_values = lax.all_gather(scaled, "tile", axis=0, tiled=True)
    total = jnp.dot(
        same, piece_values.reshape(-1, width), preferred_element_type=jnp.float32
    )
    picked = (total / count[:, None]).astype(jnp.bfloat16).reshape(values.shape)
    return (root[..., None] * (spatial + picked.astype(jnp.float32))).astype(jnp.bfloat16)


def local(features, cotangent, weight_first, weight_second, cluster_id, cluster_size):
    feats = features[0]
    band_rows, grid_cols, in_width = feats.shape
    hidden_width = weight_first.shape[1]
    out_width = weight_second.shape[1]
    members = cluster_id[0].reshape(-1)
    every = lax.all_gather(members, "tile", axis=0, tiled=True)
    same = (members[:, None] == every[None, :]).astype(jnp.bfloat16)
    count = jnp.take(cluster_size[0], members).astype(jnp.float32)
    flat_in = feats.reshape(-1, in_width)
    hidden_in = jnp.dot(flat_in, weight_first, preferred_element_type=jnp.float32).astype(
        jnp.bfloat16
    )
    hidden_grid = hidden_in.reshape(band_rows, grid_cols, hidden_width)
    pre_act = propagate(hidden_grid, same, count)
    back_second = propagate(cotangent[0], same, count)
    pre_flat = pre_act.reshape(-1, hidden_width).astype(jnp.float32)
    sigma = jax.nn.sigmoid(pre_flat)
    activated = (pre_flat * sigma).astype(jnp.bfloat16)
    back_flat = back_second.reshape(-1, out_width)
    grad_second = lax.dot_general(
        activated, back_flat, (((0,), (0,)), ((), ())), preferred_element_type=jnp.float32
    )
    upstream = lax.dot_general(
        back_flat, weight_second, (((1,), (1,)), ((), ())), preferred_element_type=jnp.float32
    )
    grad_pre = (upstream * sigma * (1.0 + pre_flat * (1.0 - sigma))).astype(jnp.bfloat16)
    back_first = propagate(
        grad_pre.reshape(band_rows, grid_cols, hidden_width), same, count
    )
    first_flat = back_first.reshape(-1, hidden_width)
    grad_first = lax.dot_general(
        flat_in, first_flat, (((0,), (0,)), ((), ())), preferred_element_type=jnp.float32
    )
    grad_feats = lax.dot_general(
        first_flat, weight_first, (((1,), (1,)), ((), ())), preferred_element_type=jnp.float32
    ).astype(jnp.bfloat16)
    grad_first, grad_second = lax.psum(
        (grad_first.astype(jnp.bfloat16), grad_second.astype(jnp.bfloat16)), ("dp", "tile")
    )
    return (
        grad_feats.reshape(1, band_rows, grid_cols, in_width),
        grad_first.astype(jnp.float32),
        grad_second.astype(jnp.float32),
    )


F32, BF16 = jnp.float32, jnp.bfloat16
MESH = pl.DeviceIdType.MESH
NT = (((1,), (1,)), ((), ()))
TN = (((0,), (0,)), ((), ()))


def dot(a, b, dims=(((1,), (0,)), ((), ()))):
    return lax.dot_general(a, b, dims, preferred_element_type=F32)


def lanes(table, width):
    return jnp.concatenate([table] * (width // 128), axis=1)


def kernel(
    x_ref, c_ref, w1_ref, w2_ref, id_ref, out_ref, gf_ref, gs_ref,
    ids, same, rcnt, sc, sh, sg, hs, back, act, tot, ups, first, fsend,
    gf, gs, gfb, gsb, gfr, gsr, gfx, gfxr, gfz, gsz, gfzr, gszr, sends, recvs,
):
    t = lax.axis_index("tile")
    z = lax.axis_index("dp")
    x, c = t // 2, t % 2
    other = (1 - x) * 2 + c
    core = x * 2 + (1 - c)
    diag = (1 - x) * 2 + (1 - c)
    zs = [lax.rem(z + d, 4) for d in (1, 2, 3)]
    barrier = pltpu.get_barrier_semaphore()
    for peer in (other, core, diag):
        pl.semaphore_signal(barrier, inc=1, device_id={"tile": peer}, device_id_type=MESH)
    for peer in zs:
        pl.semaphore_signal(barrier, inc=1, device_id={"dp": peer}, device_id_type=MESH)

    used = [0]
    pending = []

    def send(src, dst, where, track=True):
        k = used[0]
        used[0] += 1
        copy = pltpu.make_async_remote_copy(
            src_ref=src, dst_ref=dst, send_sem=sends.at[k], recv_sem=recvs.at[k],
            device_id=where, device_id_type=MESH,
        )
        copy.start()
        if track:
            pending.append(copy)
        return copy

    def flush():
        for copy in pending:
            copy.wait_send()
        pending.clear()

    col = lax.broadcasted_iota(jnp.int32, (128, 128), 0)
    cp = jnp.where((col == 0) | (col == 127), 2.0, 3.0).astype(F32)

    def root_of(i):
        rp = jnp.where((i == 0) | (i == 31), 2.0, 3.0)
        return 1.0 / jnp.sqrt(rp * cp + 1.0)

    def q_of(i):
        inside = (i >= 0) & (i <= 31)
        return jnp.where(inside, jnp.where((i == 0) | (i == 31), 0.5, 1.0 / 3.0), 0.0)

    def grid_rows(ref, i, count=1):
        return ref.at[pl.ds(pl.multiple_of((i + 2) * 128, 128), 128 * count), :]

    ids[pl.ds(pl.multiple_of(t * 8, 8), 8), :] = id_ref[...]

    def scale_c(r, _):
        i = t * 8 + r
        v = c_ref[pl.ds(pl.multiple_of(r * 128, 128), 128), :].astype(F32)
        sc[pl.ds(pl.multiple_of((i + 2) * 128, 128), 128), :] = (
            v * lanes(root_of(i), 512)
        ).astype(BF16)
        return 0

    lax.fori_loop(0, 8, scale_c, 0)
    for ref in (sc, sh, sg):
        ref[0:256, :] = jnp.zeros((256, ref.shape[1]), BF16)
        ref[4352:4608, :] = jnp.zeros((256, ref.shape[1]), BF16)

    pl.semaphore_wait(barrier, 6)
    mine = ids.at[pl.ds(pl.multiple_of(t * 8, 8), 8), :]
    id_copies = [send(mine, mine, {"tile": p}) for p in (other, core, diag)]
    cx = []
    for part in range(4):
        block = grid_rows(sc, t * 8 + part * 2, 2)
        cx.append(send(block, block, {"tile": other}, False))
    own = grid_rows(sc, t * 8, 8)
    c_core = send(own, own, {"tile": core})

    def hidden(g, _):
        rows = pl.ds(pl.multiple_of(g * 256, 256), 256)
        for j in range(2):
            hv = dot(x_ref[rows, :], w1_ref[:, j * 256 : j * 256 + 256]).astype(BF16)
            for k in range(2):
                i = t * 8 + g * 2 + k
                s = hv[k * 128 : k * 128 + 128].astype(F32) * lanes(root_of(i), 256)
                hs[j, pl.ds(pl.multiple_of(g * 256 + k * 128, 128), 128), :] = s.astype(BF16)
        return 0

    lax.fori_loop(0, 4, hidden, 0)
    rows_h = grid_rows(sh, t * 8, 8)
    h_core = send(hs.at[x], rows_h, {"tile": core})
    sh[pl.ds(pl.multiple_of((t * 8 + 2) * 128, 128), 1024), :] = hs[x]

    for copy in id_copies:
        copy.wait_recv()

    def build(rr, _):
        band = (rr // 8) * 2 + c
        row = ids[pl.ds(band * 8 + rr % 8, 1), :].astype(F32)
        tall = jnp.transpose(jnp.broadcast_to(row, (128, 128)))
        acc = jnp.zeros((128, 128), F32)
        dst = pl.ds(pl.multiple_of(rr * 128, 128), 128)
        for k in range(32):
            v = jnp.where(tall == ids[k : k + 1, :].astype(F32), 1.0, 0.0)
            acc = acc + v
            same[dst, k * 128 : k * 128 + 128] = v.astype(BF16)
        rcnt[dst, :] = jnp.broadcast_to(1.0 / jnp.sum(acc, axis=1, keepdims=True), (128, 128))
        return 0

    lax.fori_loop(0, 16, build, 0)

    def prop(src, width, xb, emit, before=None):
        def group(g, _):
            rows = pl.ds(pl.multiple_of(xb * 1024 + g * 512, 512), 512)
            tot[:, :width] = dot(same[rows, :], src[256:4352, :])
            if before is not None:
                before(rows)

            def one(r, _):
                lr = g * 4 + r
                i = (xb * 2 + c) * 8 + lr
                qs = [q_of(i - 1), q_of(i), q_of(i + 1)]
                taps = [qs[0], qs[0] + qs[1], qs[0] + qs[1] + qs[2], qs[1] + qs[2], qs[2]]
                local = pl.ds(pl.multiple_of(r * 128, 128), 128)
                at = pl.ds(pl.multiple_of(xb * 1024 + lr * 128, 128), 128)
                root = root_of(i)
                for w in range(0, width, 256):
                    ch = slice(w, w + 256)
                    v = jnp.zeros((128, 256), F32)
                    for k in range(5):
                        rowk = src[pl.ds(pl.multiple_of((i + k) * 128, 128), 128), ch]
                        v = v + taps[k] * rowk.astype(F32)
                    colw = lanes(col, 256)

                    def colbox(u):
                        up = jnp.where(colw == 0, 0.0, pltpu.roll(u, 1, 0))
                        down = jnp.where(colw == 127, 0.0, pltpu.roll(u, 127, 0))
                        return u + up + down

                    v = colbox(colbox(v) * lanes(1.0 / cp, 256))
                    mean = (tot[local, ch] * lanes(rcnt[at, :], 256)).astype(BF16)
                    emit(lr, i, at, local, ch, root, lanes(root, 256) * (v + mean.astype(F32)))
                return 0

            lax.fori_loop(0, 4, one, 0)
            return 0

        lax.fori_loop(0, 2, group, 0)

    fw = []
    for part in range(4):
        cx[part].wait_recv()
        block = grid_rows(sc, other * 8 + part * 2, 2)
        fw.append(send(block, block, {"tile": core}))
    for part in range(4):
        cx[part].wait_send()
    h_x = send(hs.at[1 - x], rows_h, {"tile": other})
    c_core.wait_recv()
    for copy in fw:
        copy.wait_recv()

    def emit_c(lr, i, at, local, ch, root, value):
        back[at, ch] = value.astype(BF16)

    prop(sc, 512, 0, emit_c)
    prop(sc, 512, 1, emit_c)

    h_x.wait_recv()
    block = grid_rows(sh, other * 8, 8)
    h_fw = send(block, block, {"tile": core})
    h_core.wait_recv()
    h_fw.wait_recv()

    def before_h(rows):
        half = w2_ref[pl.ds(pl.multiple_of(x * 256, 256), 256), :]
        ups[...] = dot(back[rows, :], half, NT)

    def emit_h(lr, i, at, local, ch, root, value):
        p = value.astype(BF16).astype(F32)
        sig = 1.0 / (1.0 + jnp.exp(-p))
        act[at, :] = (p * sig).astype(BF16)
        g = (ups[local, :] * sig * (1.0 + p * (1.0 - sig))).astype(BF16)
        sg[pl.ds(pl.multiple_of((i + 2) * 128, 128), 128), :] = (
            g.astype(F32) * lanes(root, 256)
        ).astype(BF16)

    g_core = []
    for xb in range(2):
        prop(sh, 256, xb, emit_h, before_h)
        block = grid_rows(sg, (xb * 2 + c) * 8, 8)
        g_core.append(send(block, block, {"tile": core}))
    gs[...] = dot(act[...], back[...], TN)
    for copy in g_core:
        copy.wait_recv()

    def emit_send(lr, i, at, local, ch, root, value):
        fsend[pl.ds(pl.multiple_of(lr * 128, 128), 128), :] = value.astype(BF16)

    def emit_keep(lr, i, at, local, ch, root, value):
        first[x, pl.ds(pl.multiple_of(lr * 128, 128), 128), :] = value.astype(BF16)

    prop(sg, 256, 1 - x, emit_send)
    f_x = send(fsend, first.at[x], {"tile": other})
    prop(sg, 256, x, emit_keep)

    def xt(j):
        def step(g, _):
            rows = pl.ds(pl.multiple_of(g * 256, 256), 256)
            gf[j, rows, :] = dot(x_ref[:, pl.ds(pl.multiple_of(g * 256, 256), 256)], first[j], TN)
            return 0

        lax.fori_loop(0, 4, step, 0)

    xt(x)
    f_x.wait_recv()
    xt(1 - x)

    up, low = (1 - c) * 512, c * 512
    gfb[...] = gf[:, pl.ds(pl.multiple_of(up, 512), 512), :].astype(BF16)
    gsb[...] = gs[pl.ds(pl.multiple_of((1 - c) * 128, 128), 128), :].astype(BF16)
    s1 = send(gfb, gfr, {"tile": core})
    s2 = send(gsb, gsr, {"tile": core})

    def feats(g, _):
        rows = pl.ds(pl.multiple_of(g * 256, 256), 256)
        out_ref[rows, :] = (
            dot(first[0, rows, :], w1_ref[:, 0:256], NT)
            + dot(first[1, rows, :], w1_ref[:, 256:512], NT)
        ).astype(BF16)
        return 0

    s1.wait_recv()
    s2.wait_recv()
    theirs = pl.multiple_of(low + (1 - x) * 256, 256)
    ours = pl.multiple_of(low + x * 256, 256)
    rtheirs = pl.multiple_of((1 - x) * 256, 256)
    rours = pl.multiple_of(x * 256, 256)
    gfx[...] = (
        gf[:, pl.ds(theirs, 256), :] + gfr[:, pl.ds(rtheirs, 256), :].astype(F32)
    ).astype(BF16)
    s3 = send(gfx, gfxr, {"tile": other})
    gs_mine = gs[pl.ds(pl.multiple_of(c * 128, 128), 128), :] + gsr[...].astype(F32)
    gsz[...] = gs_mine.astype(BF16)
    s4 = []
    for k, peer in enumerate(zs):
        s4.append(
            send(gsz.at[pl.ds(pl.multiple_of(peer * 32, 32), 32), :], gszr.at[k], {"dp": peer})
        )
    lax.fori_loop(0, 4, feats, 0)
    s3.wait_recv()
    gf[:, pl.ds(ours, 256), :] = (
        gf[:, pl.ds(ours, 256), :]
        + gfr[:, pl.ds(rours, 256), :].astype(F32)
        + gfxr[...].astype(F32)
    )
    gfz[...] = gf[:, pl.ds(ours, 256), :].astype(BF16)
    s5 = []
    for k, peer in enumerate(zs):
        s5.append(
            send(gfz.at[:, pl.ds(pl.multiple_of(peer * 64, 64), 64), :], gfzr.at[k], {"dp": peer})
        )
    for copy in s4:
        copy.wait_recv()
    srow = pl.multiple_of(z * 32, 32)
    total = gsz[pl.ds(srow, 32), :].astype(F32)
    for k in range(3):
        total = total + gszr[k].astype(F32)
    gs_at = pl.multiple_of(x * 256 + c * 128, 128)
    gs_ref[pl.ds(pl.multiple_of(gs_at + z * 32, 32), 32), :] = total.astype(BF16)
    piece = gs_ref.at[pl.ds(pl.multiple_of(gs_at + z * 32, 32), 32), :]
    s6 = [send(piece, piece, {"dp": peer}) for peer in zs]
    for copy in s5:
        copy.wait_recv()
    total = gf[:, pl.ds(pl.multiple_of(ours + z * 64, 64), 64), :]
    for k in range(3):
        total = total + gfzr[k].astype(F32)
    gf_ref[:, pl.ds(pl.multiple_of(ours + z * 64, 64), 64), :] = total.astype(BF16)
    piece = gf_ref.at[:, pl.ds(pl.multiple_of(ours + z * 64, 64), 64), :]
    s7 = [send(piece, piece, {"dp": peer}) for peer in zs]
    for copy in s6:
        copy.wait_recv()
    piece = gs_ref.at[pl.ds(gs_at, 128), :]
    s8 = send(piece, piece, {"tile": other})
    for copy in s7:
        copy.wait_recv()
    piece = gf_ref.at[:, pl.ds(ours, 256), :]
    s9 = send(piece, piece, {"tile": other})
    s8.wait_recv()
    s10 = []
    for xb in range(2):
        piece = gs_ref.at[pl.ds(pl.multiple_of(xb * 256 + c * 128, 128), 128), :]
        s10.append(send(piece, piece, {"tile": core}))
    s9.wait_recv()
    piece = gf_ref.at[:, pl.ds(pl.multiple_of(low, 512), 512), :]
    s11 = send(piece, piece, {"tile": core})
    for copy in s10:
        copy.wait_recv()
    s11.wait_recv()
    flush()


def fused(features, cotangent, weight_first, weight_second, cluster_id, cluster_size):
    vm = pltpu.VMEM
    scratch = [
        vm((32, 128), jnp.int32), vm((2048, 4096), BF16), vm((2048, 128), F32),
        vm((4608, 512), BF16), vm((4608, 256), BF16), vm((4608, 256), BF16),
        vm((2, 1024, 256), BF16), vm((2048, 512), BF16), vm((2048, 256), BF16),
        vm((512, 512), F32), vm((512, 256), F32), vm((2, 1024, 256), BF16),
        vm((1024, 256), BF16), vm((2, 1024, 256), F32), vm((256, 512), F32),
        vm((2, 512, 256), BF16), vm((128, 512), BF16), vm((2, 512, 256), BF16),
        vm((128, 512), BF16), vm((2, 256, 256), BF16), vm((2, 256, 256), BF16),
        vm((2, 256, 256), BF16), vm((128, 512), BF16), vm((3, 2, 64, 256), BF16),
        vm((3, 32, 512), BF16), pltpu.SemaphoreType.DMA((40,)), pltpu.SemaphoreType.DMA((40,)),
    ]
    spec = pl.BlockSpec(memory_space=pltpu.VMEM)
    feats, first, second = pl.pallas_call(
        kernel,
        out_shape=(
            jax.ShapeDtypeStruct((1024, 1024), BF16),
            jax.ShapeDtypeStruct((2, 1024, 256), BF16),
            jax.ShapeDtypeStruct((512, 512), BF16),
        ),
        in_specs=[spec] * 5,
        out_specs=(spec,) * 3,
        scratch_shapes=scratch,
        compiler_params=pltpu.CompilerParams(
            collective_id=0, has_side_effects=True, vmem_limit_bytes=60 * 1024 * 1024
        ),
    )(
        features.reshape(1024, 1024), cotangent.reshape(1024, 512),
        weight_first, weight_second, cluster_id[0],
    )
    grad_first = jnp.concatenate([first[0], first[1]], axis=1).astype(F32)
    return feats.reshape(features.shape), grad_first, second.astype(F32)


def solution(mesh):
    in_specs = (
        P(("groups", "dp"), "tile", None, None),
        P(("groups", "dp"), "tile", None, None),
        P(),
        P(),
        P(("groups", "dp"), "tile", None),
        P(("groups", "dp"), None),
    )
    out_specs = (P(("groups", "dp"), "tile", None, None), P("groups", None), P("groups", None))
    sized = mesh.shape["tile"] == 4 and mesh.shape["dp"] == 4
    body = fused if sized else local
    return jax.shard_map(body, mesh=mesh, in_specs=in_specs, out_specs=out_specs, check_vma=False)
```

```python
import jax
import jax.numpy as jnp
from jax import lax
from jax.experimental import pallas as pl
from jax.experimental.pallas import tpu as pltpu
from jax.sharding import PartitionSpec as P


def extended(cells, sides, width):
    for axis, dim in sides:
        count = lax.axis_size(axis)
        ends = count - 1
        head = lax.slice_in_dim(cells, 0, width, axis=dim)
        tail = lax.slice_in_dim(cells, cells.shape[dim] - width, cells.shape[dim], axis=dim)
        cells = jnp.concatenate(
            [
                lax.ppermute(tail, axis, [(i, (i + 1) % count) for i in range(ends)]),
                cells,
                lax.ppermute(head, axis, [((i + 1) % count, i) for i in range(ends)]),
            ],
            axis=dim,
        )
    return cells


def rowbox(values):
    return values[:-2] + values[1:-1] + values[2:]


def colbox(values):
    padded = jnp.pad(values, ((0, 0), (1, 1), (0, 0)))
    return padded[:, :-2] + padded[:, 1:-1] + padded[:, 2:]


def spread_rows(global_rows, row_total, col_total):
    row_part = (
        3.0
        - (global_rows == 0).astype(jnp.float32)
        - (global_rows == row_total - 1).astype(jnp.float32)
    )
    col_index = jnp.arange(col_total)
    col_part = (
        3.0
        - (col_index == 0).astype(jnp.float32)
        - (col_index == col_total - 1).astype(jnp.float32)
    )
    return row_part[:, None] * col_part[None, :]


def propagate(values, same, count):
    band_rows, grid_cols, width = values.shape
    bands = lax.axis_size("tile")
    row_start = lax.axis_index("tile") * band_rows
    row_total = band_rows * bands
    global_rows = row_start + jnp.arange(band_rows)
    spread = spread_rows(global_rows, row_total, grid_cols)
    root = 1.0 / jnp.sqrt(spread + 1.0)
    scaled = (values.astype(jnp.float32) * root[..., None]).astype(jnp.bfloat16)
    padded = extended(scaled, (("tile", 0),), 1)
    spatial_mean = colbox(rowbox(padded.astype(jnp.float32))) / spread[..., None]
    widened = extended(spatial_mean, (("tile", 0),), 1)
    spatial = colbox(rowbox(widened))
    piece_values = lax.all_gather(scaled, "tile", axis=0, tiled=True)
    total = jnp.dot(
        same, piece_values.reshape(-1, width), preferred_element_type=jnp.float32
    )
    picked = (total / count[:, None]).astype(jnp.bfloat16).reshape(values.shape)
    return (root[..., None] * (spatial + picked.astype(jnp.float32))).astype(jnp.bfloat16)


def local(features, cotangent, weight_first, weight_second, cluster_id, cluster_size):
    feats = features[0]
    band_rows, grid_cols, in_width = feats.shape
    hidden_width = weight_first.shape[1]
    out_width = weight_second.shape[1]
    members = cluster_id[0].reshape(-1)
    every = lax.all_gather(members, "tile", axis=0, tiled=True)
    same = (members[:, None] == every[None, :]).astype(jnp.bfloat16)
    count = jnp.take(cluster_size[0], members).astype(jnp.float32)
    flat_in = feats.reshape(-1, in_width)
    hidden_in = jnp.dot(flat_in, weight_first, preferred_element_type=jnp.float32).astype(
        jnp.bfloat16
    )
    hidden_grid = hidden_in.reshape(band_rows, grid_cols, hidden_width)
    pre_act = propagate(hidden_grid, same, count)
    back_second = propagate(cotangent[0], same, count)
    pre_flat = pre_act.reshape(-1, hidden_width).astype(jnp.float32)
    sigma = jax.nn.sigmoid(pre_flat)
    activated = (pre_flat * sigma).astype(jnp.bfloat16)
    back_flat = back_second.reshape(-1, out_width)
    grad_second = lax.dot_general(
        activated, back_flat, (((0,), (0,)), ((), ())), preferred_element_type=jnp.float32
    )
    upstream = lax.dot_general(
        back_flat, weight_second, (((1,), (1,)), ((), ())), preferred_element_type=jnp.float32
    )
    grad_pre = (upstream * sigma * (1.0 + pre_flat * (1.0 - sigma))).astype(jnp.bfloat16)
    back_first = propagate(
        grad_pre.reshape(band_rows, grid_cols, hidden_width), same, count
    )
    first_flat = back_first.reshape(-1, hidden_width)
    grad_first = lax.dot_general(
        flat_in, first_flat, (((0,), (0,)), ((), ())), preferred_element_type=jnp.float32
    )
    grad_feats = lax.dot_general(
        first_flat, weight_first, (((1,), (1,)), ((), ())), preferred_element_type=jnp.float32
    ).astype(jnp.bfloat16)
    grad_first, grad_second = lax.psum(
        (grad_first.astype(jnp.bfloat16), grad_second.astype(jnp.bfloat16)), ("dp", "tile")
    )
    return (
        grad_feats.reshape(1, band_rows, grid_cols, in_width),
        grad_first.astype(jnp.float32),
        grad_second.astype(jnp.float32),
    )


F32, BF16 = jnp.float32, jnp.bfloat16
MESH = pl.DeviceIdType.MESH
NT = (((1,), (1,)), ((), ()))
TN = (((0,), (0,)), ((), ()))


def dot(a, b, dims=(((1,), (0,)), ((), ()))):
    return lax.dot_general(a, b, dims, preferred_element_type=F32)


def lanes(table, width):
    return jnp.concatenate([table] * (width // 128), axis=1)


def kernel(
    x_ref, c_ref, w1_ref, w2_ref, id_ref, out_ref, gf_ref, gs_ref,
    ids, same, rcnt, sc, sh, sg, hs, back, act, slope, first, fsend,
    gf, gs, gfb, gsb, gfr, gsr, gfx, gfxr, gfz, gsz, gfzr, gszr, sends, recvs,
):
    t = lax.axis_index("tile")
    z = lax.axis_index("dp")
    x, c = t // 2, t % 2
    other = (1 - x) * 2 + c
    core = x * 2 + (1 - c)
    diag = (1 - x) * 2 + (1 - c)
    zs = [lax.rem(z + d, 4) for d in (1, 2, 3)]
    barrier = pltpu.get_barrier_semaphore()
    for peer in (other, core, diag):
        pl.semaphore_signal(barrier, inc=1, device_id={"tile": peer}, device_id_type=MESH)
    for peer in zs:
        pl.semaphore_signal(barrier, inc=1, device_id={"dp": peer}, device_id_type=MESH)

    used = [0]
    pending = []

    def send(src, dst, where, track=True):
        k = used[0]
        used[0] += 1
        copy = pltpu.make_async_remote_copy(
            src_ref=src, dst_ref=dst, send_sem=sends.at[k], recv_sem=recvs.at[k],
            device_id=where, device_id_type=MESH,
        )
        copy.start()
        if track:
            pending.append(copy)
        return copy

    def flush():
        for copy in pending:
            copy.wait_send()
        pending.clear()

    col = lax.broadcasted_iota(jnp.int32, (128, 128), 0)
    cp = jnp.where((col == 0) | (col == 127), 2.0, 3.0).astype(F32)

    def root_of(i):
        rp = jnp.where((i == 0) | (i == 31), 2.0, 3.0)
        return 1.0 / jnp.sqrt(rp * cp + 1.0)

    def q_of(i):
        inside = (i >= 0) & (i <= 31)
        return jnp.where(inside, jnp.where((i == 0) | (i == 31), 0.5, 1.0 / 3.0), 0.0)

    def grid_rows(ref, i, count=1):
        return ref.at[pl.ds(pl.multiple_of((i + 2) * 128, 128), 128 * count), :]

    ids[pl.ds(pl.multiple_of(t * 8, 8), 8), :] = id_ref[...]

    def scale_c(r, _):
        i = t * 8 + r
        v = c_ref[pl.ds(pl.multiple_of(r * 128, 128), 128), :].astype(F32)
        v = (v * lanes(root_of(i), 512)).astype(BF16)
        for j in range(2):
            sc[j, pl.ds(pl.multiple_of((i + 2) * 128, 128), 128), :] = v[:, j * 256 : j * 256 + 256]
        return 0

    lax.fori_loop(0, 8, scale_c, 0)
    for ref in (sc.at[0], sc.at[1], sh, sg):
        ref[0:256, :] = jnp.zeros((256, ref.shape[1]), BF16)
        ref[4352:4608, :] = jnp.zeros((256, ref.shape[1]), BF16)

    pl.semaphore_wait(barrier, 6)
    mine = ids.at[pl.ds(pl.multiple_of(t * 8, 8), 8), :]
    id_copies = [send(mine, mine, {"tile": p}) for p in (other, core, diag)]
    def send_c(j, where, band, track=True):
        blocks = [grid_rows(sc.at[j], band * 8 + part * 4, 4) for part in range(2)]
        return [send(block, block, {"tile": where}, track) for block in blocks]

    cx = send_c(0, other, t, False)
    c_core = send_c(0, core, t) + send_c(1, core, t)

    def hidden(g, _):
        rows = pl.ds(pl.multiple_of(g * 256, 256), 256)
        for j in range(2):
            hv = dot(x_ref[rows, :], w1_ref[:, j * 256 : j * 256 + 256]).astype(BF16)
            for k in range(2):
                i = t * 8 + g * 2 + k
                s = hv[k * 128 : k * 128 + 128].astype(F32) * lanes(root_of(i), 256)
                hs[j, pl.ds(pl.multiple_of(g * 256 + k * 128, 128), 128), :] = s.astype(BF16)
        return 0

    lax.fori_loop(0, 4, hidden, 0)
    rows_h = grid_rows(sh, t * 8, 8)
    h_core = send(hs.at[x], rows_h, {"tile": core})
    h_x = send(hs.at[1 - x], rows_h, {"tile": other})
    sh[pl.ds(pl.multiple_of((t * 8 + 2) * 128, 128), 1024), :] = hs[x]

    for copy in id_copies:
        copy.wait_recv()

    def build(rr, _):
        band = (rr // 8) * 2 + c
        row = ids[pl.ds(band * 8 + rr % 8, 1), :].astype(F32)
        tall = jnp.transpose(jnp.broadcast_to(row, (128, 128)))
        acc = jnp.zeros((128, 128), F32)
        dst = pl.ds(pl.multiple_of(rr * 128, 128), 128)
        for k in range(32):
            v = jnp.where(tall == ids[k : k + 1, :].astype(F32), 1.0, 0.0)
            acc = acc + v
            same[dst, k * 128 : k * 128 + 128] = v.astype(BF16)
        rcnt[dst, :] = jnp.broadcast_to(1.0 / jnp.sum(acc, axis=1, keepdims=True), (128, 128))
        return 0

    lax.fori_loop(0, 16, build, 0)

    def prop_group(src, xb, g, emit):
        total = dot(same[pl.ds(pl.multiple_of(xb * 1024 + g * 512, 512), 512), :], src[256:4352, :])
        colw = lanes(col, 256)

        def colbox(u):
            up = jnp.where(colw == 0, 0.0, pltpu.roll(u, 1, 0))
            down = jnp.where(colw == 127, 0.0, pltpu.roll(u, 127, 0))
            return u + up + down

        for r in range(4):
            lr = g * 4 + r
            i = (xb * 2 + c) * 8 + lr
            qs = [q_of(i - 1), q_of(i), q_of(i + 1)]
            taps = [qs[0], qs[0] + qs[1], qs[0] + qs[1] + qs[2], qs[1] + qs[2], qs[2]]
            at = pl.ds(pl.multiple_of(xb * 1024 + lr * 128, 128), 128)
            v = jnp.zeros((128, 256), F32)
            for k in range(5):
                rowk = src[pl.ds(pl.multiple_of((i + k) * 128, 128), 128), :]
                v = v + taps[k] * rowk.astype(F32)
            v = colbox(colbox(v) * lanes(1.0 / cp, 256))
            mean = (total[r * 128 : r * 128 + 128] * lanes(rcnt[at, :], 256)).astype(BF16)
            emit(lr, i, at, lanes(root_of(i), 256) * (v + mean.astype(F32)))

    def prop(src, xb, emit):
        def group(g, _):
            prop_group(src, xb, g, emit)
            return 0

        lax.fori_loop(0, 2, group, 0)

    def prop_both(src, emit):
        def group(g, _):
            prop_group(src, g // 2, g % 2, emit)
            return 0

        lax.fori_loop(0, 4, group, 0)

    def forward_c(j, copies):
        out = []
        for part in range(2):
            copies[part].wait_recv()
            block = grid_rows(sc.at[j], other * 8 + part * 4, 4)
            out.append(send(block, block, {"tile": core}))
        for copy in out:
            copy.wait_recv()

    for copy in cx:
        copy.wait_send()
    cy = send_c(1, other, t)
    for copy in c_core:
        copy.wait_recv()
    forward_c(0, cx)

    def emit_c(j):
        def emit(lr, i, at, value):
            back[at, j * 256 : j * 256 + 256] = value.astype(BF16)

        return emit

    prop_both(sc.at[0], emit_c(0))
    h_x.wait_recv()
    block = grid_rows(sh, other * 8, 8)
    h_fw = send(block, block, {"tile": core})
    h_core.wait_recv()
    h_fw.wait_recv()

    def emit_h(lr, i, at, value):
        p = value.astype(BF16).astype(F32)
        sig = 1.0 / (1.0 + jnp.exp(-p))
        act[at, :] = (p * sig).astype(BF16)
        slope[at, :] = sig * (1.0 + p * (1.0 - sig))

    prop_both(sh, emit_h)
    forward_c(1, cy)

    def upstream(xb):
        half = w2_ref[pl.ds(pl.multiple_of(x * 256, 256), 256), :]

        def step(g, _):
            rows = pl.ds(pl.multiple_of(xb * 1024 + g * 256, 256), 256)
            grad = (dot(back[rows, :], half, NT) * slope[rows, :]).astype(BF16).astype(F32)
            for k in range(2):
                i = (xb * 2 + c) * 8 + g * 2 + k
                sg[pl.ds(pl.multiple_of((i + 2) * 128, 128), 128), :] = (
                    grad[k * 128 : k * 128 + 128] * lanes(root_of(i), 256)
                ).astype(BF16)
            return 0

        lax.fori_loop(0, 4, step, 0)

    g_core = []
    for xb in range(2):
        prop(sc.at[1], xb, emit_c(1))
        upstream(xb)
        block = grid_rows(sg, (xb * 2 + c) * 8, 8)
        g_core.append(send(block, block, {"tile": core}))
    gs[...] = dot(act[...], back[...], TN)
    for copy in g_core:
        copy.wait_recv()

    def emit_send(lr, i, at, value):
        fsend[pl.ds(pl.multiple_of(lr * 128, 128), 128), :] = value.astype(BF16)

    def emit_keep(lr, i, at, value):
        first[x, pl.ds(pl.multiple_of(lr * 128, 128), 128), :] = value.astype(BF16)

    f_x = []
    for g in range(2):
        prop_group(sg, 1 - x, g, emit_send)
        part = pl.ds(g * 512, 512)
        f_x.append(send(fsend.at[part, :], first.at[x, part, :], {"tile": other}))
    prop(sg, x, emit_keep)

    def xt(j):
        def step(g, _):
            rows = pl.ds(pl.multiple_of(g * 256, 256), 256)
            gf[j, rows, :] = dot(x_ref[:, pl.ds(pl.multiple_of(g * 256, 256), 256)], first[j], TN)
            return 0

        lax.fori_loop(0, 4, step, 0)

    xt(x)
    for copy in f_x:
        copy.wait_recv()
    xt(1 - x)

    up, low = (1 - c) * 512, c * 512
    gfb[...] = gf[:, pl.ds(pl.multiple_of(up, 512), 512), :].astype(BF16)
    gsb[...] = gs[pl.ds(pl.multiple_of((1 - c) * 128, 128), 128), :].astype(BF16)
    s1 = send(gfb, gfr, {"tile": core})
    s2 = send(gsb, gsr, {"tile": core})

    def feats(g, _):
        rows = pl.ds(pl.multiple_of(g * 256, 256), 256)
        out_ref[rows, :] = (
            dot(first[0, rows, :], w1_ref[:, 0:256], NT)
            + dot(first[1, rows, :], w1_ref[:, 256:512], NT)
        ).astype(BF16)
        return 0

    s1.wait_recv()
    s2.wait_recv()
    theirs = pl.multiple_of(low + (1 - x) * 256, 256)
    ours = pl.multiple_of(low + x * 256, 256)
    rtheirs = pl.multiple_of((1 - x) * 256, 256)
    rours = pl.multiple_of(x * 256, 256)
    gfx[...] = (
        gf[:, pl.ds(theirs, 256), :] + gfr[:, pl.ds(rtheirs, 256), :].astype(F32)
    ).astype(BF16)
    s3 = send(gfx, gfxr, {"tile": other})
    gs_mine = gs[pl.ds(pl.multiple_of(c * 128, 128), 128), :] + gsr[...].astype(F32)
    gsz[...] = gs_mine.astype(BF16)
    s4 = []
    for k, peer in enumerate(zs):
        s4.append(
            send(gsz.at[pl.ds(pl.multiple_of(peer * 32, 32), 32), :], gszr.at[k], {"dp": peer})
        )
    lax.fori_loop(0, 4, feats, 0)
    s3.wait_recv()
    gf[:, pl.ds(ours, 256), :] = (
        gf[:, pl.ds(ours, 256), :]
        + gfr[:, pl.ds(rours, 256), :].astype(F32)
        + gfxr[...].astype(F32)
    )
    gfz[...] = gf[:, pl.ds(ours, 256), :].astype(BF16)
    s5 = []
    for k, peer in enumerate(zs):
        s5.append(
            send(gfz.at[:, pl.ds(pl.multiple_of(peer * 64, 64), 64), :], gfzr.at[k], {"dp": peer})
        )
    for copy in s4:
        copy.wait_recv()
    srow = pl.multiple_of(z * 32, 32)
    total = gsz[pl.ds(srow, 32), :].astype(F32)
    for k in range(3):
        total = total + gszr[k].astype(F32)
    gs_at = pl.multiple_of(x * 256 + c * 128, 128)
    gs_ref[pl.ds(pl.multiple_of(gs_at + z * 32, 32), 32), :] = total.astype(BF16)
    piece = gs_ref.at[pl.ds(pl.multiple_of(gs_at + z * 32, 32), 32), :]
    s6 = [send(piece, piece, {"dp": peer}) for peer in zs]
    for copy in s5:
        copy.wait_recv()
    total = gf[:, pl.ds(pl.multiple_of(ours + z * 64, 64), 64), :]
    for k in range(3):
        total = total + gfzr[k].astype(F32)
    gf_ref[pl.ds(pl.multiple_of(ours + z * 64, 64), 64), :] = jnp.concatenate(
        [total[0], total[1]], axis=1
    ).astype(BF16)
    piece = gf_ref.at[pl.ds(pl.multiple_of(ours + z * 64, 64), 64), :]
    s7 = [send(piece, piece, {"dp": peer}) for peer in zs]
    for copy in s6:
        copy.wait_recv()
    piece = gs_ref.at[pl.ds(gs_at, 128), :]
    s8 = send(piece, piece, {"tile": other})
    for copy in s7:
        copy.wait_recv()
    piece = gf_ref.at[pl.ds(ours, 256), :]
    s9 = send(piece, piece, {"tile": other})
    s8.wait_recv()
    s10 = []
    for xb in range(2):
        piece = gs_ref.at[pl.ds(pl.multiple_of(xb * 256 + c * 128, 128), 128), :]
        s10.append(send(piece, piece, {"tile": core}))
    s9.wait_recv()
    piece = gf_ref.at[pl.ds(pl.multiple_of(low, 512), 512), :]
    s11 = send(piece, piece, {"tile": core})
    for copy in s10:
        copy.wait_recv()
    s11.wait_recv()
    flush()


def fused(features, cotangent, weight_first, weight_second, cluster_id, cluster_size):
    vm = pltpu.VMEM
    scratch = [
        vm((32, 128), jnp.int32), vm((2048, 4096), BF16), vm((2048, 128), F32),
        vm((2, 4608, 256), BF16), vm((4608, 256), BF16), vm((4608, 256), BF16),
        vm((2, 1024, 256), BF16), vm((2048, 512), BF16), vm((2048, 256), BF16),
        vm((2048, 256), F32), vm((2, 1024, 256), BF16),
        vm((1024, 256), BF16), vm((2, 1024, 256), F32), vm((256, 512), F32),
        vm((2, 512, 256), BF16), vm((128, 512), BF16), vm((2, 512, 256), BF16),
        vm((128, 512), BF16), vm((2, 256, 256), BF16), vm((2, 256, 256), BF16),
        vm((2, 256, 256), BF16), vm((128, 512), BF16), vm((3, 2, 64, 256), BF16),
        vm((3, 32, 512), BF16), pltpu.SemaphoreType.DMA((48,)), pltpu.SemaphoreType.DMA((48,)),
    ]
    spec = pl.BlockSpec(memory_space=pltpu.VMEM)
    feats, first, second = pl.pallas_call(
        kernel,
        out_shape=(
            jax.ShapeDtypeStruct((1024, 1024), BF16),
            jax.ShapeDtypeStruct((1024, 512), BF16),
            jax.ShapeDtypeStruct((512, 512), BF16),
        ),
        in_specs=[spec] * 5,
        out_specs=(spec,) * 3,
        scratch_shapes=scratch,
        compiler_params=pltpu.CompilerParams(
            collective_id=0, has_side_effects=True, vmem_limit_bytes=60 * 1024 * 1024
        ),
    )(
        features.reshape(1024, 1024), cotangent.reshape(1024, 512),
        weight_first, weight_second, cluster_id[0],
    )
    return feats.reshape(features.shape), first.astype(F32), second.astype(F32)


def solution(mesh):
    in_specs = (
        P(("groups", "dp"), "tile", None, None),
        P(("groups", "dp"), "tile", None, None),
        P(),
        P(),
        P(("groups", "dp"), "tile", None),
        P(("groups", "dp"), None),
    )
    out_specs = (P(("groups", "dp"), "tile", None, None), P("groups", None), P("groups", None))
    sized = mesh.shape["tile"] == 4 and mesh.shape["dp"] == 4
    body = fused if sized else local
    return jax.shard_map(body, mesh=mesh, in_specs=in_specs, out_specs=out_specs, check_vma=False)
```

```python
import jax
import jax.numpy as jnp
from jax import lax
from jax.experimental import pallas as pl
from jax.experimental.pallas import tpu as pltpu
from jax.sharding import PartitionSpec as P


def extended(cells, sides, width):
    for axis, dim in sides:
        count = lax.axis_size(axis)
        ends = count - 1
        head = lax.slice_in_dim(cells, 0, width, axis=dim)
        tail = lax.slice_in_dim(cells, cells.shape[dim] - width, cells.shape[dim], axis=dim)
        cells = jnp.concatenate(
            [
                lax.ppermute(tail, axis, [(i, (i + 1) % count) for i in range(ends)]),
                cells,
                lax.ppermute(head, axis, [((i + 1) % count, i) for i in range(ends)]),
            ],
            axis=dim,
        )
    return cells


def rowbox(values):
    return values[:-2] + values[1:-1] + values[2:]


def colbox(values):
    padded = jnp.pad(values, ((0, 0), (1, 1), (0, 0)))
    return padded[:, :-2] + padded[:, 1:-1] + padded[:, 2:]


def spread_rows(global_rows, row_total, col_total):
    row_part = (
        3.0
        - (global_rows == 0).astype(jnp.float32)
        - (global_rows == row_total - 1).astype(jnp.float32)
    )
    col_index = jnp.arange(col_total)
    col_part = (
        3.0
        - (col_index == 0).astype(jnp.float32)
        - (col_index == col_total - 1).astype(jnp.float32)
    )
    return row_part[:, None] * col_part[None, :]


def propagate(values, same, count):
    band_rows, grid_cols, width = values.shape
    bands = lax.axis_size("tile")
    row_start = lax.axis_index("tile") * band_rows
    row_total = band_rows * bands
    global_rows = row_start + jnp.arange(band_rows)
    spread = spread_rows(global_rows, row_total, grid_cols)
    root = 1.0 / jnp.sqrt(spread + 1.0)
    scaled = (values.astype(jnp.float32) * root[..., None]).astype(jnp.bfloat16)
    padded = extended(scaled, (("tile", 0),), 1)
    spatial_mean = colbox(rowbox(padded.astype(jnp.float32))) / spread[..., None]
    widened = extended(spatial_mean, (("tile", 0),), 1)
    spatial = colbox(rowbox(widened))
    piece_values = lax.all_gather(scaled, "tile", axis=0, tiled=True)
    total = jnp.dot(
        same, piece_values.reshape(-1, width), preferred_element_type=jnp.float32
    )
    picked = (total / count[:, None]).astype(jnp.bfloat16).reshape(values.shape)
    return (root[..., None] * (spatial + picked.astype(jnp.float32))).astype(jnp.bfloat16)


def local(features, cotangent, weight_first, weight_second, cluster_id, cluster_size):
    feats = features[0]
    band_rows, grid_cols, in_width = feats.shape
    hidden_width = weight_first.shape[1]
    out_width = weight_second.shape[1]
    members = cluster_id[0].reshape(-1)
    every = lax.all_gather(members, "tile", axis=0, tiled=True)
    same = (members[:, None] == every[None, :]).astype(jnp.bfloat16)
    count = jnp.take(cluster_size[0], members).astype(jnp.float32)
    flat_in = feats.reshape(-1, in_width)
    hidden_in = jnp.dot(flat_in, weight_first, preferred_element_type=jnp.float32).astype(
        jnp.bfloat16
    )
    hidden_grid = hidden_in.reshape(band_rows, grid_cols, hidden_width)
    pre_act = propagate(hidden_grid, same, count)
    back_second = propagate(cotangent[0], same, count)
    pre_flat = pre_act.reshape(-1, hidden_width).astype(jnp.float32)
    sigma = jax.nn.sigmoid(pre_flat)
    activated = (pre_flat * sigma).astype(jnp.bfloat16)
    back_flat = back_second.reshape(-1, out_width)
    grad_second = lax.dot_general(
        activated, back_flat, (((0,), (0,)), ((), ())), preferred_element_type=jnp.float32
    )
    upstream = lax.dot_general(
        back_flat, weight_second, (((1,), (1,)), ((), ())), preferred_element_type=jnp.float32
    )
    grad_pre = (upstream * sigma * (1.0 + pre_flat * (1.0 - sigma))).astype(jnp.bfloat16)
    back_first = propagate(
        grad_pre.reshape(band_rows, grid_cols, hidden_width), same, count
    )
    first_flat = back_first.reshape(-1, hidden_width)
    grad_first = lax.dot_general(
        flat_in, first_flat, (((0,), (0,)), ((), ())), preferred_element_type=jnp.float32
    )
    grad_feats = lax.dot_general(
        first_flat, weight_first, (((1,), (1,)), ((), ())), preferred_element_type=jnp.float32
    ).astype(jnp.bfloat16)
    grad_first, grad_second = lax.psum(
        (grad_first.astype(jnp.bfloat16), grad_second.astype(jnp.bfloat16)), ("dp", "tile")
    )
    return (
        grad_feats.reshape(1, band_rows, grid_cols, in_width),
        grad_first.astype(jnp.float32),
        grad_second.astype(jnp.float32),
    )


F32, BF16 = jnp.float32, jnp.bfloat16
MESH = pl.DeviceIdType.MESH
NT = (((1,), (1,)), ((), ()))
TN = (((0,), (0,)), ((), ()))


def dot(a, b, dims=(((1,), (0,)), ((), ()))):
    return lax.dot_general(a, b, dims, preferred_element_type=F32)


def lanes(table, width):
    return jnp.concatenate([table] * (width // 128), axis=1)


def kernel(
    x_ref, c_ref, w1_ref, w2_ref, id_ref, out_ref, gf_ref, gs_ref,
    ids, same, rcnt, sc, sh, sg, hs, back, act, slope, first, fsend,
    gf, gs, gfb, gsb, gfr, gsr, gfx, gfxr, gfz, gsz, gfzr, gszr, sends, recvs,
):
    t = lax.axis_index("tile")
    z = lax.axis_index("dp")
    x, c = t // 2, t % 2
    other = (1 - x) * 2 + c
    core = x * 2 + (1 - c)
    diag = (1 - x) * 2 + (1 - c)
    zs = [lax.rem(z + d, 4) for d in (1, 2, 3)]
    barrier = pltpu.get_barrier_semaphore()
    for peer in (other, core, diag):
        pl.semaphore_signal(barrier, inc=1, device_id={"tile": peer}, device_id_type=MESH)
    for peer in zs:
        pl.semaphore_signal(barrier, inc=1, device_id={"dp": peer}, device_id_type=MESH)

    used = [0]
    pending = []

    def send(src, dst, where, track=True):
        k = used[0]
        used[0] += 1
        copy = pltpu.make_async_remote_copy(
            src_ref=src, dst_ref=dst, send_sem=sends.at[k], recv_sem=recvs.at[k],
            device_id=where, device_id_type=MESH,
        )
        copy.start()
        if track:
            pending.append(copy)
        return copy

    def flush():
        for copy in pending:
            copy.wait_send()
        pending.clear()

    col = lax.broadcasted_iota(jnp.int32, (128, 128), 0)
    cp = jnp.where((col == 0) | (col == 127), 2.0, 3.0).astype(F32)

    def root_of(i):
        rp = jnp.where((i == 0) | (i == 31), 2.0, 3.0)
        return 1.0 / jnp.sqrt(rp * cp + 1.0)

    def q_of(i):
        inside = (i >= 0) & (i <= 31)
        return jnp.where(inside, jnp.where((i == 0) | (i == 31), 0.5, 1.0 / 3.0), 0.0)

    def grid_rows(ref, i, count=1):
        return ref.at[pl.ds(pl.multiple_of((i + 2) * 128, 128), 128 * count), :]

    ids[pl.ds(pl.multiple_of(t * 8, 8), 8), :] = id_ref[...]

    def scale_c(r, _):
        i = t * 8 + r
        v = c_ref[pl.ds(pl.multiple_of(r * 128, 128), 128), :].astype(F32)
        v = (v * lanes(root_of(i), 512)).astype(BF16)
        for j in range(2):
            sc[j, pl.ds(pl.multiple_of((i + 2) * 128, 128), 128), :] = v[:, j * 256 : j * 256 + 256]
        return 0

    lax.fori_loop(0, 8, scale_c, 0)
    for ref in (sc.at[0], sc.at[1], sh, sg):
        ref[0:256, :] = jnp.zeros((256, ref.shape[1]), BF16)
        ref[4352:4608, :] = jnp.zeros((256, ref.shape[1]), BF16)

    pl.semaphore_wait(barrier, 6)
    mine = ids.at[pl.ds(pl.multiple_of(t * 8, 8), 8), :]
    id_copies = [send(mine, mine, {"tile": p}) for p in (other, core, diag)]
    def send_c(j, where, band, track=True):
        blocks = [grid_rows(sc.at[j], band * 8 + part * 4, 4) for part in range(2)]
        return [send(block, block, {"tile": where}, track) for block in blocks]

    cx = send_c(0, other, t, False)
    c_core = send_c(0, core, t) + send_c(1, core, t)

    def hidden(g, _):
        rows = pl.ds(pl.multiple_of(g * 256, 256), 256)
        for j in range(2):
            hv = dot(x_ref[rows, :], w1_ref[:, j * 256 : j * 256 + 256]).astype(BF16)
            for k in range(2):
                i = t * 8 + g * 2 + k
                s = hv[k * 128 : k * 128 + 128].astype(F32) * lanes(root_of(i), 256)
                hs[j, pl.ds(pl.multiple_of(g * 256 + k * 128, 128), 128), :] = s.astype(BF16)
        return 0

    lax.fori_loop(0, 4, hidden, 0)
    rows_h = grid_rows(sh, t * 8, 8)
    h_core = send(hs.at[x], rows_h, {"tile": core})
    h_x = send(hs.at[1 - x], rows_h, {"tile": other})
    sh[pl.ds(pl.multiple_of((t * 8 + 2) * 128, 128), 1024), :] = hs[x]

    for copy in id_copies:
        copy.wait_recv()

    def build(rr, _):
        band = (rr // 8) * 2 + c
        row = ids[pl.ds(band * 8 + rr % 8, 1), :].astype(F32)
        tall = jnp.transpose(jnp.broadcast_to(row, (128, 128)))
        acc = jnp.zeros((128, 128), F32)
        dst = pl.ds(pl.multiple_of(rr * 128, 128), 128)
        for k in range(32):
            v = jnp.where(tall == ids[k : k + 1, :].astype(F32), 1.0, 0.0)
            acc = acc + v
            same[dst, k * 128 : k * 128 + 128] = v.astype(BF16)
        rcnt[dst, :] = jnp.broadcast_to(1.0 / jnp.sum(acc, axis=1, keepdims=True), (128, 128))
        return 0

    lax.fori_loop(0, 16, build, 0)

    def prop_group(src, xb, g, emit):
        total = dot(same[pl.ds(pl.multiple_of(xb * 1024 + g * 512, 512), 512), :], src[256:4352, :])
        colw = lanes(col, 256)

        def colbox(u):
            up = jnp.where(colw == 0, 0.0, pltpu.roll(u, 1, 0))
            down = jnp.where(colw == 127, 0.0, pltpu.roll(u, 127, 0))
            return u + up + down

        for r in range(4):
            lr = g * 4 + r
            i = (xb * 2 + c) * 8 + lr
            qs = [q_of(i - 1), q_of(i), q_of(i + 1)]
            taps = [qs[0], qs[0] + qs[1], qs[0] + qs[1] + qs[2], qs[1] + qs[2], qs[2]]
            at = pl.ds(pl.multiple_of(xb * 1024 + lr * 128, 128), 128)
            v = jnp.zeros((128, 256), F32)
            for k in range(5):
                rowk = src[pl.ds(pl.multiple_of((i + k) * 128, 128), 128), :]
                v = v + taps[k] * rowk.astype(F32)
            v = colbox(colbox(v) * lanes(1.0 / cp, 256))
            mean = (total[r * 128 : r * 128 + 128] * lanes(rcnt[at, :], 256)).astype(BF16)
            emit(lr, i, at, lanes(root_of(i), 256) * (v + mean.astype(F32)))

    def prop(src, xb, emit):
        def group(g, _):
            prop_group(src, xb, g, emit)
            return 0

        lax.fori_loop(0, 2, group, 0)

    def prop_both(src, emit):
        def group(g, _):
            prop_group(src, g // 2, g % 2, emit)
            return 0

        lax.fori_loop(0, 4, group, 0)

    def forward_c(j, copies):
        out = []
        for part in range(2):
            copies[part].wait_recv()
            block = grid_rows(sc.at[j], other * 8 + part * 4, 4)
            out.append(send(block, block, {"tile": core}))
        for copy in out:
            copy.wait_recv()

    for copy in cx:
        copy.wait_send()
    cy = send_c(1, other, t)
    for copy in c_core:
        copy.wait_recv()
    forward_c(0, cx)

    def emit_c(j):
        def emit(lr, i, at, value):
            back[at, j * 256 : j * 256 + 256] = value.astype(BF16)

        return emit

    prop_both(sc.at[0], emit_c(0))
    h_x.wait_recv()
    block = grid_rows(sh, other * 8, 8)
    h_fw = send(block, block, {"tile": core})
    h_core.wait_recv()
    h_fw.wait_recv()

    def emit_h(lr, i, at, value):
        p = value.astype(BF16).astype(F32)
        sig = 1.0 / (1.0 + jnp.exp(-p))
        act[at, :] = (p * sig).astype(BF16)
        slope[at, :] = sig * (1.0 + p * (1.0 - sig))

    prop_both(sh, emit_h)
    forward_c(1, cy)

    def upstream(xb):
        half = w2_ref[pl.ds(pl.multiple_of(x * 256, 256), 256), :]

        def step(g, _):
            rows = pl.ds(pl.multiple_of(xb * 1024 + g * 256, 256), 256)
            grad = (dot(back[rows, :], half, NT) * slope[rows, :]).astype(BF16).astype(F32)
            for k in range(2):
                i = (xb * 2 + c) * 8 + g * 2 + k
                sg[pl.ds(pl.multiple_of((i + 2) * 128, 128), 128), :] = (
                    grad[k * 128 : k * 128 + 128] * lanes(root_of(i), 256)
                ).astype(BF16)
            return 0

        lax.fori_loop(0, 4, step, 0)

    g_core = []
    for xb in range(2):
        prop(sc.at[1], xb, emit_c(1))
        upstream(xb)
        block = grid_rows(sg, (xb * 2 + c) * 8, 8)
        g_core.append(send(block, block, {"tile": core}))
    gs[...] = dot(act[...], back[...], TN)
    gsb[...] = gs[pl.ds(pl.multiple_of((1 - c) * 128, 128), 128), :].astype(BF16)
    s2 = send(gsb, gsr, {"tile": core})
    for copy in g_core:
        copy.wait_recv()
    s2.wait_recv()
    gs_mine = gs[pl.ds(pl.multiple_of(c * 128, 128), 128), :] + gsr[...].astype(F32)
    gsz[...] = gs_mine.astype(BF16)
    s4 = []
    for k, peer in enumerate(zs):
        s4.append(
            send(gsz.at[pl.ds(pl.multiple_of(peer * 32, 32), 32), :], gszr.at[k], {"dp": peer})
        )

    def emit_send(lr, i, at, value):
        fsend[pl.ds(pl.multiple_of(lr * 128, 128), 128), :] = value.astype(BF16)

    def emit_keep(lr, i, at, value):
        first[x, pl.ds(pl.multiple_of(lr * 128, 128), 128), :] = value.astype(BF16)

    f_x = []
    for g in range(2):
        prop_group(sg, 1 - x, g, emit_send)
        part = pl.ds(g * 512, 512)
        f_x.append(send(fsend.at[part, :], first.at[x, part, :], {"tile": other}))
    for copy in s4:
        copy.wait_recv()
    total = gsz[pl.ds(pl.multiple_of(z * 32, 32), 32), :].astype(F32)
    for k in range(3):
        total = total + gszr[k].astype(F32)
    gs_at = pl.multiple_of(x * 256 + c * 128, 128)
    gs_ref[pl.ds(pl.multiple_of(gs_at + z * 32, 32), 32), :] = total.astype(BF16)
    piece = gs_ref.at[pl.ds(pl.multiple_of(gs_at + z * 32, 32), 32), :]
    s6 = [send(piece, piece, {"dp": peer}) for peer in zs]
    prop(sg, x, emit_keep)
    for copy in s6:
        copy.wait_recv()
    piece = gs_ref.at[pl.ds(gs_at, 128), :]
    s8 = send(piece, piece, {"tile": other})

    def xt(j):
        def step(g, _):
            rows = pl.ds(pl.multiple_of(g * 256, 256), 256)
            gf[j, rows, :] = dot(x_ref[:, pl.ds(pl.multiple_of(g * 256, 256), 256)], first[j], TN)
            return 0

        lax.fori_loop(0, 4, step, 0)

    xt(x)
    for copy in f_x:
        copy.wait_recv()
    xt(1 - x)

    up, low = (1 - c) * 512, c * 512
    s1 = []
    for j in range(2):
        gfb[j] = gf[j, pl.ds(pl.multiple_of(up, 512), 512), :].astype(BF16)
        s1.append(send(gfb.at[j], gfr.at[j], {"tile": core}))

    def feats(g, _):
        rows = pl.ds(pl.multiple_of(g * 256, 256), 256)
        out_ref[rows, :] = (
            dot(first[0, rows, :], w1_ref[:, 0:256], NT)
            + dot(first[1, rows, :], w1_ref[:, 256:512], NT)
        ).astype(BF16)
        return 0

    theirs = pl.ds(pl.multiple_of(low + (1 - x) * 256, 256), 256)
    ours = pl.ds(pl.multiple_of(low + x * 256, 256), 256)
    rtheirs = pl.ds(pl.multiple_of((1 - x) * 256, 256), 256)
    rours = pl.ds(pl.multiple_of(x * 256, 256), 256)
    s3 = []
    for j in range(2):
        s1[j].wait_recv()
        gfx[j] = (gf[j, theirs, :] + gfr[j, rtheirs, :].astype(F32)).astype(BF16)
        s3.append(send(gfx.at[j], gfxr.at[j], {"tile": other}))
    s8.wait_recv()
    s10 = []
    for xb in range(2):
        piece = gs_ref.at[pl.ds(pl.multiple_of(xb * 256 + c * 128, 128), 128), :]
        s10.append(send(piece, piece, {"tile": core}))
    lax.fori_loop(0, 2, feats, 0)
    s5 = []
    for j in range(2):
        s3[j].wait_recv()
        gf[j, ours, :] = (
            gf[j, ours, :] + gfr[j, rours, :].astype(F32) + gfxr[j].astype(F32)
        )
        gfz[j] = gf[j, ours, :].astype(BF16)
        for k, peer in enumerate(zs):
            part = pl.ds(pl.multiple_of(peer * 64, 64), 64)
            s5.append(send(gfz.at[j, part, :], gfzr.at[k, j], {"dp": peer}))
    lax.fori_loop(2, 4, feats, 0)
    here = pl.ds(pl.multiple_of(low + x * 256 + z * 64, 64), 64)
    s7 = []
    for j in range(2):
        ch = slice(j * 256, j * 256 + 256)
        for copy in s5[j * 3 : j * 3 + 3]:
            copy.wait_recv()
        total = gf[j, here, :]
        for k in range(3):
            total = total + gfzr[k, j].astype(F32)
        gf_ref[here, ch] = total.astype(BF16)
        piece = gf_ref.at[here, ch]
        s7.append([send(piece, piece, {"dp": peer}) for peer in zs])
    s9 = []
    for j in range(2):
        for copy in s7[j]:
            copy.wait_recv()
        piece = gf_ref.at[ours, j * 256 : j * 256 + 256]
        s9.append(send(piece, piece, {"tile": other}))
    s11 = []
    for j in range(2):
        piece = gf_ref.at[ours, j * 256 : j * 256 + 256]
        s11.append(send(piece, piece, {"tile": core}))
    for j in range(2):
        s9[j].wait_recv()
        piece = gf_ref.at[theirs, j * 256 : j * 256 + 256]
        s11.append(send(piece, piece, {"tile": core}))
    for copy in s10 + s11:
        copy.wait_recv()
    flush()


def fused(features, cotangent, weight_first, weight_second, cluster_id, cluster_size):
    vm = pltpu.VMEM
    scratch = [
        vm((32, 128), jnp.int32), vm((2048, 4096), BF16), vm((2048, 128), F32),
        vm((2, 4608, 256), BF16), vm((4608, 256), BF16), vm((4608, 256), BF16),
        vm((2, 1024, 256), BF16), vm((2048, 512), BF16), vm((2048, 256), BF16),
        vm((2048, 256), F32), vm((2, 1024, 256), BF16),
        vm((1024, 256), BF16), vm((2, 1024, 256), F32), vm((256, 512), F32),
        vm((2, 512, 256), BF16), vm((128, 512), BF16), vm((2, 512, 256), BF16),
        vm((128, 512), BF16), vm((2, 256, 256), BF16), vm((2, 256, 256), BF16),
        vm((2, 256, 256), BF16), vm((128, 512), BF16), vm((3, 2, 64, 256), BF16),
        vm((3, 32, 512), BF16), pltpu.SemaphoreType.DMA((64,)), pltpu.SemaphoreType.DMA((64,)),
    ]
    spec = pl.BlockSpec(memory_space=pltpu.VMEM)
    feats, first, second = pl.pallas_call(
        kernel,
        out_shape=(
            jax.ShapeDtypeStruct((1024, 1024), BF16),
            jax.ShapeDtypeStruct((1024, 512), BF16),
            jax.ShapeDtypeStruct((512, 512), BF16),
        ),
        in_specs=[spec] * 5,
        out_specs=(spec,) * 3,
        scratch_shapes=scratch,
        compiler_params=pltpu.CompilerParams(
            collective_id=0, has_side_effects=True, vmem_limit_bytes=60 * 1024 * 1024
        ),
    )(
        features.reshape(1024, 1024), cotangent.reshape(1024, 512),
        weight_first, weight_second, cluster_id[0],
    )
    return feats.reshape(features.shape), first.astype(F32), second.astype(F32)


def solution(mesh):
    in_specs = (
        P(("groups", "dp"), "tile", None, None),
        P(("groups", "dp"), "tile", None, None),
        P(),
        P(),
        P(("groups", "dp"), "tile", None),
        P(("groups", "dp"), None),
    )
    out_specs = (P(("groups", "dp"), "tile", None, None), P("groups", None), P("groups", None))
    sized = mesh.shape["tile"] == 4 and mesh.shape["dp"] == 4
    body = fused if sized else local
    return jax.shard_map(body, mesh=mesh, in_specs=in_specs, out_specs=out_specs, check_vma=False)
```
